128 devices in a mesh: grp: 4 (over y), seq: 32 (over z, x, core).
Axes of the slice: x: 4, y: 4, z: 4, core: 2. Of those that a mesh axis runs over, the one named last changes fastest.
Arguments:
- byte_ids: int32 [4, 4096], P('grp', 'seq'), may hold values from 0 to 255
- patch_lengths: int32 [4, 256], P('grp'), may hold values from 1 to 32, 4096 in all within a row
- patch_owner: int32 [4, 256], P('grp'), may hold values from 0 to 31, as said below
- emb_table: bfloat16 [256, 1024], replicated, may hold values from -6 to 6
- enc_gain: float32 [1024], replicated, may hold values from 0.1 to 1.9
- w_in: bfloat16 [1024, 4096], P(None, 'seq'), may hold values from -0.1875 to 0.1875
- lat_gain: float32 [4096], replicated, may hold values from 0.1 to 1.9
- w_gate: bfloat16 [14336, 4096], P(('grp', 'seq')), may hold values from -0.09375 to 0.09375
- w_up: bfloat16 [14336, 4096], P(('grp', 'seq')), may hold values from -0.09375 to 0.09375
- w_down: bfloat16 [14336, 4096], P(('grp', 'seq')), may hold values from -0.046875 to 0.046875
- grad_out: bfloat16 [4, 32, 8, 4096], P('grp', 'seq'), may hold values from -6 to 6
Outputs:
- patch_out: bfloat16 [4, 32, 8, 4096], P('grp', 'seq')
- d_emb: float32 [256, 1024], replicated
- d_enc_gain: float32 [1024], replicated
- d_w_in: float32 [1024, 4096], P(None, 'seq')
- d_lat_gain: float32 [4096], replicated
- d_w_gate: float32 [14336, 4096], P(('grp', 'seq'))
- d_w_up: float32 [14336, 4096], P(('grp', 'seq'))
- d_w_down: float32 [14336, 4096], P(('grp', 'seq'))
The draws below stay inside these ranges and needn't reach their ends.
Inputs may be any that keep to these rules, and one draw needn't show every extreme that they name: `patch_owner`: in each sequence every owner number appears exactly 8 times. `patch_lengths`: each sequence's lengths sum to 4096; the longest is exactly 32.
All inputs are finite; a program needn't handle non-finite values.
Results may differ from the reference program's by a relative error of at most 0.02.
Values may be sent and summed in bfloat16 or wider, within the bound.
No kernel may reach another device: no remote copies, remote signals or barrier semaphores. Data moves between devices by JAX's collectives and lax.ppermute only.
A program may use at most 192 MiB of HBM per device.

```python
import math
import jax
import jax.numpy as jnp
import numpy as np
from jax import lax

ENC_D = 1024
LAT_D = 4096
LAT_FF = 14336
VOCAB = 256
PATCH_DEV = 8
GROUPS = 4
GROUP_BYTES = 4096
PATCHES = 256
MOST = 32
N_SEQ = 32


def draw_patch_owner(key, part):
    key = jax.random.fold_in(key, 7)
    keys = jax.random.split(key, GROUPS)
    orders = jax.vmap(lambda single: jax.random.permutation(single, PATCHES))(keys)
    return (orders // PATCH_DEV).astype(jnp.int32)


def with_ends(drawn, key, smallest, largest):
    dims = drawn.shape
    index_at = [jax.random.randint(jax.random.fold_in(key, axis), (), 0, dims[axis]) for axis in range(len(dims))]
    drawn = drawn.at[tuple(index_at)].set(smallest)
    longest = dims.index(max(dims))
    index_at[longest] = (index_at[longest] + 1) % dims[longest]
    return drawn.at[tuple(index_at)].set(largest)


def steps_of(rng, extent, shards, smallest, top_value):
    factor_of, own = 1.0, jax.random.fold_in(rng, 6)
    for dim, blocks in shards:
        draws = jnp.exp(jax.random.uniform(jax.random.fold_in(own, dim), (blocks,), jnp.float32, smallest / len(shards), top_value / len(shards)))
        factor_of = factor_of * jnp.repeat(draws, extent[dim] // blocks).reshape([-1 if axis == dim else 1 for axis in range(len(extent))])
    return factor_of


def cumulative_ranks(amount, skew):
    loads = [(1 << 20) // math.isqrt(grade ** skew) + 1 for grade in range(1, amount + 1)]
    scale = 1 + sum(loads) // (1 << 30)
    return np.cumsum(np.array([max(1, weight // scale) for weight in loads]))


def ranked_ids(own_key, shape, number_of, skew):
    table = cumulative_ranks(number_of, skew)
    pick = jax.random.randint(jax.random.fold_in(own_key, 1), shape, 0, int(table[number_of - 1]))
    grade = jnp.searchsorted(jnp.asarray(table, jnp.int32), pick, side="right")
    return jax.random.permutation(jax.random.fold_in(own_key, 2), number_of)[grade].astype(jnp.int32)


def profile(count, total, bound, skew):
    weights = [(1 << 20) // math.isqrt(grade ** skew) + 1 for grade in range(2, count + 1)]
    spare, counts = total - bound - (count - 1), [1] * (count - 1)
    while spare > 0:
        candidates = [i for i in range(count - 1) if counts[i] < bound]
        pool, remaining = sum([weights[i] for i in candidates]), spare
        for i in candidates:
            addition = min(bound - counts[i], max(1, remaining * weights[i] // pool), spare)
            counts[i] = counts[i] + addition
            spare = spare - addition
    return np.array([bound] + counts)


def uneven_parts(stream_key, count, total, reach, skew):
    if count == 2:
        one = jax.random.randint(stream_key, (), max(1, total - reach), min(reach, total - 1) + 1)
        return jnp.stack([one, total - one])
    sizes = jnp.asarray(profile(count, total, reach, skew), jnp.int32)
    couples = (count - 1) // 2
    source_of, sink = sizes[1:1 + 2 * couples:2], sizes[2:2 + 2 * couples:2]
    slack = jnp.minimum(source_of - 1, reach - sink)
    moved = jax.random.randint(jax.random.fold_in(stream_key, 1), (couples,), 0, 1 << 20) % (slack + 1)
    sizes = sizes.at[1:1 + 2 * couples:2].set(source_of - moved).at[2:2 + 2 * couples:2].set(sink + moved)
    return sizes[jax.random.permutation(jax.random.fold_in(stream_key, 2), count)]


def noise(own_key, extent, scale, bound, cuts=(), held_as=jnp.bfloat16):
    values = jax.random.normal(own_key, extent, jnp.float32) * scale
    if len(cuts) > 0:
        values = steps_of(own_key, extent, cuts, -0.22, 0.18) * values
    return jnp.clip(values, min=-bound, max=bound).astype(held_as)


def setup_inputs(seed: int = 0) -> dict:
    streams_of = jax.random.split(jax.random.key(seed), 12)
    return {
        "byte_ids": with_ends(ranked_ids(streams_of[0], (GROUPS, GROUP_BYTES), VOCAB, 1), jax.random.fold_in(streams_of[0], 3), 0, VOCAB - 1).astype(jnp.int32),
        "patch_lengths": jax.vmap(lambda own: uneven_parts(own, PATCHES, GROUP_BYTES, MOST, 2))(jax.random.split(streams_of[1], GROUPS)).reshape((GROUPS, PATCHES)).astype(jnp.int32),
        "patch_owner": draw_patch_owner(jax.random.fold_in(streams_of[11], 71), 0),
        "emb_table": noise(streams_of[3], (VOCAB, ENC_D), 1.0, 6.0),
        "enc_gain": jnp.clip(1.0 + 0.18 * jax.random.normal(streams_of[4], (ENC_D,), jnp.float32), 0.1, 1.9),
        "w_in": noise(streams_of[5], (ENC_D, LAT_D), ENC_D ** -0.5, 0.1875, ((1, 32),)),
        "lat_gain": jnp.clip(1.0 + 0.18 * jax.random.normal(streams_of[6], (LAT_D,), jnp.float32), 0.1, 1.9),
        "w_gate": noise(streams_of[7], (LAT_FF, LAT_D), LAT_D ** -0.5, 0.09375, ((0, 128),)),
        "w_up": noise(streams_of[8], (LAT_FF, LAT_D), LAT_D ** -0.5, 0.09375, ((0, 128),)),
        "w_down": noise(streams_of[9], (LAT_FF, LAT_D), LAT_FF ** -0.5, 0.046875, ((0, 128),)),
        "grad_out": noise(streams_of[10], (GROUPS, N_SEQ, PATCH_DEV, LAT_D), 1.0, 6.0, ((0, 4), (1, 32))),
    }


def rms_scale(values):
    return lax.rsqrt(lax.optimization_barrier(jnp.mean(values * values, axis=-1, keepdims=True)) + 1e-05)

def silu_parts(gate):
    sigma = jax.nn.sigmoid(gate)
    return (gate * sigma, sigma * (1.0 + gate * (1.0 - sigma)))

def contract_last(left, right):
    return lax.dot_general(left, right, (((1,), (1,)), ((), ())), preferred_element_type=jnp.float32)

def contract_first(left, right):
    return lax.dot_general(left, right, (((0,), (0,)), ((), ())), preferred_element_type=jnp.float32)

def reference(byte_ids, patch_lengths, patch_owner, emb_table, enc_gain, w_in, lat_gain, w_gate, w_up, w_down, grad_out):
    d_emb = jnp.zeros((VOCAB, ENC_D), jnp.float32)
    d_enc = jnp.zeros((ENC_D,), jnp.float32)
    d_win = jnp.zeros((ENC_D, LAT_D), jnp.float32)
    d_lat = jnp.zeros((LAT_D,), jnp.float32)
    d_wg = jnp.zeros((LAT_FF, LAT_D), jnp.float32)
    d_wu = jnp.zeros((LAT_FF, LAT_D), jnp.float32)
    d_wd = jnp.zeros((LAT_FF, LAT_D), jnp.float32)
    outputs = []
    for group in range(GROUPS):
        ids = byte_ids[group]
        lengths = patch_lengths[group]
        owners = patch_owner[group]
        starts = jnp.cumsum(lengths) - lengths
        position = jnp.arange(GROUP_BYTES, dtype=jnp.int32)
        member = (position[None, :] >= starts[:, None]) & (position[None, :] < (starts + lengths)[:, None])
        onehot_ids = ids[:, None] == jnp.arange(VOCAB, dtype=jnp.int32)[None, :]
        embedded = jnp.dot(onehot_ids.astype(jnp.bfloat16), emb_table, preferred_element_type=jnp.float32)
        enc_rms = rms_scale(embedded)
        unit = embedded * enc_rms
        enc = (unit * enc_gain).astype(jnp.bfloat16)
        pooled_sum = jnp.dot(member.astype(jnp.bfloat16), enc, preferred_element_type=jnp.float32)
        lens_f = lengths.astype(jnp.float32)[:, None]
        pooled = (pooled_sum / lens_f).astype(jnp.bfloat16)
        latent = jnp.dot(pooled, w_in, preferred_element_type=jnp.float32).astype(jnp.bfloat16)
        lat32 = latent.astype(jnp.float32)
        lat_rms = rms_scale(lat32)
        unit_l = lat32 * lat_rms
        normed = (unit_l * lat_gain).astype(jnp.bfloat16)
        gate = contract_last(normed, w_gate)
        upper = contract_last(normed, w_up)
        active, slope = silu_parts(gate)
        hidden = (active * upper).astype(jnp.bfloat16)
        result = lat32 + jnp.dot(hidden, w_down, preferred_element_type=jnp.float32)
        onehot_own = (owners[:, None] == jnp.arange(N_SEQ, dtype=jnp.int32)[None, :]).astype(jnp.int32)
        rank = lax.optimization_barrier(jnp.sum((jnp.cumsum(onehot_own, axis=0) - onehot_own) * onehot_own, axis=1))
        target = (owners * PATCH_DEV + rank).astype(jnp.int32)
        placed = jnp.zeros((PATCHES, LAT_D), jnp.float32).at[target].set(result)
        outputs.append(placed.astype(jnp.bfloat16).reshape(N_SEQ, PATCH_DEV, LAT_D))
        cot = grad_out[group].reshape(PATCHES, LAT_D)[target]
        d_wd = d_wd + contract_first(hidden, cot)
        dhid = contract_last(cot, w_down)
        dgate = (dhid * upper * slope).astype(jnp.bfloat16)
        dup = (dhid * active).astype(jnp.bfloat16)
        d_wg = d_wg + contract_first(dgate, normed)
        d_wu = d_wu + contract_first(dup, normed)
        dnormed = jnp.dot(dgate, w_gate, preferred_element_type=jnp.float32) + jnp.dot(dup, w_up, preferred_element_type=jnp.float32)
        d_lat = d_lat + lax.optimization_barrier(jnp.sum(dnormed * unit_l, axis=0))
        scaled = dnormed * lat_gain
        dlatent = (cot.astype(jnp.float32) + lat_rms * (scaled - unit_l * lax.optimization_barrier(jnp.mean(scaled * unit_l, axis=-1, keepdims=True)))).astype(jnp.bfloat16)
        d_win = d_win + contract_first(pooled, dlatent)
        dpool = contract_last(dlatent, w_in) / lens_f
        denc = jnp.dot(member.astype(jnp.float32).T, dpool, precision=lax.Precision.HIGHEST)
        d_enc = d_enc + lax.optimization_barrier(jnp.sum(denc * unit, axis=0))
        scaled_e = denc * enc_gain
        dembedded = enc_rms * (scaled_e - unit * lax.optimization_barrier(jnp.mean(scaled_e * unit, axis=-1, keepdims=True)))
        d_emb = d_emb + jnp.dot(onehot_ids.astype(jnp.float32).T, dembedded, precision=lax.Precision.HIGHEST)
    patch_out = jnp.stack(outputs, axis=0)
    return (patch_out, d_emb, d_enc, d_win, d_lat, d_wg, d_wu, d_wd)
```

```python
import jax
import jax.numpy as jnp
from jax import lax
from jax.sharding import Mesh, PartitionSpec as P

CHIPS = ("y", "z", "x")
ALL = ("y", "z", "x", "c")
bf16 = jnp.bfloat16
f32 = jnp.float32


def rms_scale(values):
    return lax.rsqrt(jnp.mean(values * values, axis=-1, keepdims=True) + 1e-05)


def silu_parts(gate):
    sigma = jax.nn.sigmoid(gate)
    return (gate * sigma, sigma * (1.0 + gate * (1.0 - sigma)))


def owner_slots(lengths, owners, owner_count, per_owner):
    count = lengths.shape[0]
    onehot_own = (owners[:, None] == jnp.arange(owner_count, dtype=jnp.int32)[None, :]).astype(
        jnp.int32
    )
    rank = jnp.sum((jnp.cumsum(onehot_own, axis=0) - onehot_own) * onehot_own, axis=1)
    target = owners * per_owner + rank
    placed = target[None, :] == jnp.arange(count, dtype=jnp.int32)[:, None]
    starts = jnp.cumsum(lengths) - lengths
    slot_start = jnp.sum(jnp.where(placed, starts[None, :], 0), axis=1)
    slot_len = jnp.sum(jnp.where(placed, lengths[None, :], 0), axis=1)
    return (slot_start, slot_len)


def contract_last(left, right):
    return lax.dot_general(
        left, right, (((1,), (1,)), ((), ())), preferred_element_type=f32
    )


def contract_first(left, right):
    return lax.dot_general(
        left, right, (((0,), (0,)), ((), ())), preferred_element_type=f32
    )


def slot_counts(ids, lengths, owners, vocab):
    slot_start, slot_len = owner_slots(lengths, owners, 32, 8)
    position = jnp.arange(ids.shape[0], dtype=jnp.int32)
    member = (position[None, :] >= slot_start[:, None]) & (
        position[None, :] < (slot_start + slot_len)[:, None]
    )
    onehot = ids[:, None] == jnp.arange(vocab, dtype=jnp.int32)[None, :]
    counts = jnp.dot(member.astype(bf16), onehot.astype(bf16), preferred_element_type=f32)
    return counts, slot_len


def reduce_rows(left, right, core):
    rows = left.reshape(64, 2, 8, left.shape[1])
    other = lax.dynamic_index_in_dim(rows, 1 - core, 1, keepdims=False).reshape(512, -1)
    own = lax.dynamic_index_in_dim(rows, core, 1, keepdims=False).reshape(512, -1)
    away = jnp.dot(other, right, preferred_element_type=f32).astype(bf16)
    came = lax.ppermute(away, "c", [(0, 1), (1, 0)])
    here = (jnp.dot(own, right, preferred_element_type=f32) + came.astype(f32)).astype(bf16)
    parts = lax.all_to_all(here.reshape(64, 8, -1), CHIPS, 0, 0, tiled=True)
    return jnp.sum(parts.astype(f32), axis=0)


def on_device(
    byte_ids, patch_lengths, patch_owner, emb_table, enc_gain, w_in, lat_gain,
    w_gate, w_up, w_down, grad_out,
):
    y = lax.axis_index("y")
    core = lax.axis_index("c")
    seq = lax.axis_index(("z", "x", "c"))
    vocab, width = emb_table.shape
    latd = lat_gain.shape[0]
    cot_own = grad_out[0, 0]

    tiny = jnp.concatenate(
        [
            byte_ids[0],
            lax.dynamic_slice_in_dim(patch_lengths[0], seq * 8, 8),
            lax.dynamic_slice_in_dim(patch_owner[0], seq * 8, 8),
            jnp.zeros((112,), jnp.int32),
        ]
    )
    win_quarter = lax.dynamic_slice_in_dim(w_in, y * 256, 256, 0)
    mine = jnp.concatenate([cot_own, win_quarter.reshape(8, latd)], axis=0)
    whole = lax.all_gather(mine[None], ALL, axis=0, tiled=True)
    tiny_all = lax.all_gather(tiny[None], ALL, axis=0, tiled=True)
    ids = tiny_all[:, :128].reshape(4, 4096)
    lengths = tiny_all[:, 128:136].reshape(4, 256)
    owners = tiny_all[:, 136:144].reshape(4, 256)

    embedded = emb_table.astype(f32)
    enc_rms = rms_scale(embedded)
    unit = embedded * enc_rms
    table = (unit * enc_gain).astype(bf16)
    counts, slot_len = jax.vmap(lambda i, n, o: slot_counts(i, n, o, vocab))(ids, lengths, owners)
    counts = counts.reshape(1024, vocab)
    lens = slot_len.reshape(1024, 1).astype(f32)
    pooled = (jnp.dot(counts.astype(bf16), table, preferred_element_type=f32) / lens).astype(bf16)

    cot_all = whole[:, :8].reshape(1024, latd)
    win_all = (
        whole[:, 8:].reshape(4, 32, 256, 128).transpose(0, 2, 1, 3).reshape(1024, latd)
    )
    latent = jnp.dot(pooled, win_all, preferred_element_type=f32).astype(bf16)

    lat32 = latent.astype(f32)
    normed = (lat32 * rms_scale(lat32) * lat_gain).astype(bf16)
    gate = contract_last(normed, w_gate)
    upper = contract_last(normed, w_up)
    active, slope = silu_parts(gate)
    hidden = (active * upper).astype(bf16)
    dhid = contract_last(cot_all, w_down)
    dgate = (dhid * upper * slope).astype(bf16)
    dup = (dhid * active).astype(bf16)

    dnormed = reduce_rows(
        jnp.concatenate([dgate, dup], axis=1), jnp.concatenate([w_gate, w_up], axis=0), core
    )
    mlp_own = reduce_rows(hidden, w_down, core)
    d_wd = contract_first(hidden, cot_all)
    d_wg = contract_first(dgate, normed)
    d_wu = contract_first(dup, normed)

    row0 = y * 256 + seq * 8
    own_lat = lax.dynamic_slice_in_dim(latent, row0, 8, 0).astype(f32)
    lat_rms = rms_scale(own_lat)
    unit_l = own_lat * lat_rms
    lat_part = jnp.sum(dnormed * unit_l, axis=0, keepdims=True)
    scaled = dnormed * lat_gain
    dlatent = (
        cot_own.astype(f32)
        + lat_rms * (scaled - unit_l * jnp.mean(scaled * unit_l, axis=-1, keepdims=True))
    ).astype(bf16)
    own_counts = lax.dynamic_slice_in_dim(counts, row0, 8, 0)
    own_len = lax.dynamic_slice_in_dim(lens, row0, 8, 0)
    dpool = contract_last(dlatent, win_all) / own_len
    value_part = lax.dot_general(
        own_counts, dpool, (((0,), (0,)), ((), ())), precision=lax.Precision.HIGHEST,
        preferred_element_type=f32,
    ).astype(bf16)

    columns = jnp.concatenate([dlatent, lat_part.astype(bf16)], axis=0)
    columns = columns.reshape(9, 32, 128).transpose(1, 0, 2)
    columns = jnp.broadcast_to(columns[None], (4, 32, 9, 128)).reshape(128, 9, 128)
    sent = jnp.concatenate([columns, value_part.reshape(128, 16, 128)], axis=1)
    got = lax.all_to_all(sent, ALL, 0, 0, tiled=True)
    dlat_cols = got[:, :8].reshape(1024, 128)
    d_lat_cols = jnp.sum(got[:, 8].astype(f32), axis=0)
    values = jnp.sum(got[:, 9:].astype(f32), axis=0).reshape(2, width)
    d_win = contract_first(pooled, dlat_cols)

    value0 = (y * 32 + seq) * 2
    my_unit = lax.dynamic_slice_in_dim(unit, value0, 2, 0)
    my_rms = lax.dynamic_slice_in_dim(enc_rms, value0, 2, 0)
    enc_part = jnp.sum(values * my_unit, axis=0)
    scaled_e = values * enc_gain
    d_rows = my_rms * (scaled_e - my_unit * jnp.mean(scaled_e * my_unit, axis=-1, keepdims=True))
    last = jnp.concatenate(
        [d_rows.reshape(-1), enc_part, d_lat_cols, jnp.zeros((896,), f32)]
    ).astype(bf16)
    last = jnp.broadcast_to(last.reshape(1, 32, 128), (128, 32, 128))
    ends = lax.all_to_all(last, ALL, 0, 0, tiled=True)
    d_emb = ends[:, :16].reshape(vocab, width).astype(f32)
    d_enc = jnp.sum(ends[:, 16:24].astype(f32), axis=0).reshape(width)
    d_lat = ends[:32, 24].reshape(latd).astype(f32)

    patch_out = (own_lat + mlp_own).astype(bf16).reshape(1, 1, 8, latd)
    return (patch_out, d_emb, d_enc, d_win, d_lat, d_wg, d_wu, d_wd)


def solution(mesh):
    fine = Mesh(mesh.devices.reshape(4, 4, 4, 2), ALL)
    seq = ("z", "x", "c")
    ff = P(ALL, None)
    return jax.shard_map(
        on_device,
        mesh=fine,
        in_specs=(
            P("y", seq), P("y", None), P("y", None), P(), P(), P(None, seq), P(),
            ff, ff, ff, P("y", seq, None, None),
        ),
        out_specs=(P("y", seq, None, None), P(), P(), P(None, seq), P(), ff, ff, ff),
        check_vma=False,
    )
```

```python
import jax
import jax.numpy as jnp
from jax import lax
from jax.experimental import pallas as pl
from jax.experimental.pallas import tpu as pltpu
from jax.sharding import Mesh, PartitionSpec as P

ALL = ("y", "z", "x", "c")
CHIPS = ("y", "z", "x")
SWAP = [(0, 1), (1, 0)]
EPS = 1e-05
bf16 = jnp.bfloat16
f32 = jnp.float32


def rms_scale(values):
    return lax.rsqrt(jnp.mean(values * values, axis=-1, keepdims=True) + EPS)


def silu_parts(gate):
    sigma = jax.nn.sigmoid(gate)
    return (gate * sigma, sigma * (1.0 + gate * (1.0 - sigma)))


def owner_slots(lengths, owners):
    onehot_own = (owners[:, None] == jnp.arange(32, dtype=jnp.int32)[None, :]).astype(jnp.int32)
    rank = jnp.sum((jnp.cumsum(onehot_own, axis=0) - onehot_own) * onehot_own, axis=1)
    target = owners * 8 + rank
    placed = target[None, :] == jnp.arange(256, dtype=jnp.int32)[:, None]
    starts = jnp.cumsum(lengths) - lengths
    slot_start = jnp.sum(jnp.where(placed, starts[None, :], 0), axis=1)
    slot_len = jnp.sum(jnp.where(placed, lengths[None, :], 0), axis=1)
    return (slot_start, slot_len)


def slot_counts(ids, lengths, owners, vocab):
    slot_start, slot_len = owner_slots(lengths, owners)
    position = jnp.arange(ids.shape[0], dtype=jnp.int32)
    member = (position[None, :] >= slot_start[:, None]) & (
        position[None, :] < (slot_start + slot_len)[:, None]
    )
    onehot = ids[:, None] == jnp.arange(vocab, dtype=jnp.int32)[None, :]
    counts = jnp.dot(member.astype(bf16), onehot.astype(bf16), preferred_element_type=f32)
    return counts, slot_len


def contract(left, right, left_dims, right_dims):
    return lax.dot_general(
        left, right, ((left_dims, right_dims), ((), ())), preferred_element_type=f32
    )


def first_kernel(whole, pooled, w_gu, w_dn, gain, lat_out, scaled_out, cot_out, part_out, win):
    step = pl.program_id(0)

    @pl.when(step == 0)
    def _():
        for y in range(4):
            for block in range(16):
                win[y * 256:(y + 1) * 256, block * 128:(block + 1) * 128] = (
                    whole[y * 16 + block, 0:256, :]
                )

    for chip in range(16):
        for block in range(16):
            cot_out[chip * 16:(chip + 1) * 16, block * 128:(block + 1) * 128] = (
                whole[step * 16 + chip, 256 + block * 16:272 + block * 16, :]
            )
    latent = jnp.dot(pooled[...], win[...], preferred_element_type=f32).astype(bf16)
    lat_out[...] = latent
    lat32 = latent.astype(f32)
    scaled = (lat32 * gain[...]).astype(bf16)
    scaled_out[...] = scaled
    part_out[0, 0:448, :] = contract(w_gu[...], scaled, (1,), (1,)).astype(bf16)
    part_out[0, 448:672, :] = contract(w_dn[...], cot_out[...], (1,), (1,)).astype(bf16)
    squares = contract(
        jnp.ones((16, 2048), bf16), (lat32 * lat32).astype(bf16), (1,), (1,)
    )
    high = squares.astype(bf16).astype(f32)
    top = lax.broadcasted_iota(jnp.int32, squares.shape, 0) < 8
    part_out[0, 672:688, :] = jnp.where(top, high, squares - high).astype(bf16)


def first_products(whole, pooled, w_gu, w_dn, gain):
    once = pl.Buffered(1)
    fixed = lambda *shape: pl.BlockSpec(shape, lambda i: (0,) * len(shape), pipeline_mode=once)
    rows = lambda width: pl.BlockSpec((256, width), lambda i: (i, 0))
    return pl.pallas_call(
        first_kernel,
        grid=(4,),
        in_specs=[fixed(64, 512, 128), rows(1024), fixed(448, 2048), fixed(224, 2048), fixed(1, 2048)],
        out_specs=[
            rows(2048), rows(2048), rows(2048),
            pl.BlockSpec((1, 688, 256), lambda i: (i // 2, 0, i % 2)),
            pl.BlockSpec((1024, 2048), lambda i: (0, 0), pipeline_mode=once),
        ],
        out_shape=[
            jax.ShapeDtypeStruct((1024, 2048), bf16),
            jax.ShapeDtypeStruct((1024, 2048), bf16),
            jax.ShapeDtypeStruct((1024, 2048), bf16),
            jax.ShapeDtypeStruct((2, 688, 512), bf16),
            jax.ShapeDtypeStruct((1024, 2048), bf16),
        ],
        compiler_params=pltpu.CompilerParams(vmem_limit_bytes=56 * 2**20),
        cost_estimate=pl.CostEstimate(
            flops=2 * 1024 * 2048 * (1024 + 688), bytes_accessed=30 * 2**20, transcendentals=0
        ),
    )(whole, pooled, w_gu, w_dn, gain)


def in_order(core, own, came):
    return jnp.stack([jnp.where(core == 0, own, came), jnp.where(core == 0, came, own)])


def on_device(
    byte_ids, patch_lengths, patch_owner, emb_table, enc_gain, w_in, lat_gain,
    w_gate, w_up, w_down, grad_out,
):
    y, z, x, c = (lax.axis_index(a) for a in ALL)
    chip = z * 4 + x
    seq = chip * 2 + c
    vocab, width = emb_table.shape
    latd = lat_gain.shape[0]
    mine_of = lambda a, which, axis: lax.dynamic_index_in_dim(a, which, axis, keepdims=False)

    cot_parts = grad_out[0, 0].reshape(8, 16, 2, 128)
    cot_came = lax.ppermute(mine_of(cot_parts, 1 - c, 2), "c", SWAP)
    cot_chip = in_order(c, mine_of(cot_parts, c, 2), cot_came)
    cot_chip = cot_chip.reshape(16, 16, 128).transpose(1, 0, 2).reshape(256, 128)
    win_quarter = lax.dynamic_slice_in_dim(w_in, y * 256, 256, 0)
    whole = lax.all_gather(
        jnp.concatenate([win_quarter, cot_chip], axis=0)[None], CHIPS, axis=0, tiled=True
    )

    tiny = jnp.concatenate(
        [
            byte_ids[0],
            lax.dynamic_slice_in_dim(patch_lengths[0], seq * 8, 8),
            lax.dynamic_slice_in_dim(patch_owner[0], seq * 8, 8),
            jnp.zeros((112,), jnp.int32),
        ]
    )
    tiny_all = lax.all_to_all(
        jnp.broadcast_to(tiny.reshape(1, 2, 128), (128, 2, 128)), ALL, 0, 0, tiled=True
    )
    ids = tiny_all[:, 0].reshape(4, 4096)
    lengths = tiny_all[:, 1, :8].reshape(4, 256)
    owners = tiny_all[:, 1, 8:16].reshape(4, 256)

    weights = jnp.stack([w_gate, w_up, w_down]).reshape(3, 112, 16, 2, 128)
    weights_own = mine_of(weights, c, 3).reshape(3, 112, 2048)
    weights_came = lax.ppermute(mine_of(weights, 1 - c, 3).reshape(3, 112, 2048), "c", SWAP)
    weights = in_order(c, weights_own, weights_came).transpose(1, 0, 2, 3)
    w_gu = weights[:2].reshape(448, 2048)
    w_dn = weights[2].reshape(224, 2048)

    embedded = emb_table.astype(f32)
    enc_rms = rms_scale(embedded)
    unit = embedded * enc_rms
    table = (unit * enc_gain).astype(bf16)
    counts, slot_len = jax.vmap(lambda i, n, o: slot_counts(i, n, o, vocab))(ids, lengths, owners)
    counts = counts.reshape(1024, vocab)
    lens = slot_len.reshape(1024, 1).astype(f32)
    pooled = (jnp.dot(counts.astype(bf16), table, preferred_element_type=f32) / lens).astype(bf16)
    gain = mine_of(lat_gain.reshape(16, 2, 128), c, 1).reshape(1, 2048)

    latent, scaled_lat, cot, part, win = first_products(whole, pooled, w_gu, w_dn, gain)
    part_came = lax.ppermute(mine_of(part, 1 - c, 0), "c", SWAP)
    total = mine_of(part, c, 0).astype(f32) + part_came.astype(f32)

    gate0 = total[:224]
    up0 = total[224:448]
    dhid = total[448:672]
    rms = lax.rsqrt((total[672:673] + total[680:681]) / latd + EPS)
    upper = up0 * rms
    active, slope = silu_parts(gate0 * rms)
    acts = jnp.concatenate(
        [dhid * upper * slope * rms, dhid * active * rms, active * upper], axis=0
    ).astype(bf16)
    acts = in_order(c, acts, lax.ppermute(acts, "c", SWAP))
    dgu = acts[:, :448]
    hidden = acts[:, 448:]

    dn_part = contract(dgu, w_gu, (1,), (0,)).astype(bf16)
    dn_sent = lax.all_to_all(dn_part.reshape(64, 16, 2048), CHIPS, 0, 0, tiled=True)
    mlp = contract(hidden, w_dn, (1,), (0,)).astype(bf16).reshape(1024, 2048)
    mlp = lax.psum_scatter(mlp, "y", scatter_dimension=0, tiled=True)

    d_gu = contract(dgu, scaled_lat.reshape(2, 512, 2048), (0, 2), (0, 1))
    d_dn = contract(hidden, cot.reshape(2, 512, 2048), (0, 2), (0, 1))
    d_weights = jnp.concatenate([d_gu, d_dn], axis=0).reshape(3, 2, 112, 2048)
    d_own = mine_of(d_weights, c, 1)
    d_came = lax.ppermute(mine_of(d_weights, 1 - c, 1), "c", SWAP)
    d_weights = in_order(c, d_own, d_came).reshape(2, 3, 112, 16, 128).transpose(1, 2, 3, 0, 4)
    d_wg, d_wu, d_wd = d_weights.reshape(3, 112, latd)
    dn_sent, d_wg, d_wu, d_wd = lax.optimization_barrier((dn_sent, d_wg, d_wu, d_wd))
    dnormed = jnp.sum(dn_sent.astype(f32), axis=0)

    row0 = (y * 16 + chip) * 16
    lat_own = lax.dynamic_slice_in_dim(latent, row0, 16, 0).astype(f32)
    cot_own = lax.dynamic_slice_in_dim(cot, row0, 16, 0).astype(f32)
    scaled = dnormed * gain
    sums = jnp.stack([jnp.sum(scaled * lat_own, axis=1), jnp.sum(lat_own * lat_own, axis=1)])
    sums = (sums + lax.ppermute(sums, "c", SWAP)) / latd
    mean_rows = sums[0][:, None] / (sums[1][:, None] + EPS)
    dlatent = (cot_own + scaled - lat_own * mean_rows).astype(bf16)
    d_lat_part = jnp.sum(dnormed * lat_own, axis=0)

    dpool = contract(dlatent, win, (1,), (1,)) / lax.dynamic_slice_in_dim(lens, row0, 16, 0)
    value_part = lax.dot_general(
        lax.dynamic_slice_in_dim(counts, row0, 16, 0), dpool, (((0,), (0,)), ((), ())),
        precision=lax.Precision.HIGHEST, preferred_element_type=f32,
    ).astype(bf16).reshape(2, 64, 16, 128)
    value_came = lax.ppermute(mine_of(value_part, 1 - c, 0), "c", SWAP)
    value_half = (mine_of(value_part, c, 0).astype(f32) + value_came.astype(f32)).astype(bf16)
    columns = jnp.concatenate(
        [dlatent.reshape(16, 16, 128), d_lat_part.astype(bf16).reshape(1, 16, 128)], axis=0
    ).transpose(1, 0, 2)
    columns = jnp.broadcast_to(columns[None], (4, 16, 17, 128)).reshape(64, 17, 128)
    sent = jnp.concatenate([value_half, columns], axis=1)
    sent, mlp = lax.optimization_barrier((sent, mlp))
    mlp = lax.psum_scatter(mlp, "z", scatter_dimension=0, tiled=True)
    got = lax.all_to_all(sent, CHIPS, 0, 0, tiled=True)
    values = jnp.sum(got[:, :16].astype(f32), axis=0)
    d_lat_own = jnp.sum(got[:, 32].astype(f32), axis=0)

    last = jnp.concatenate([values, d_lat_own[None]], axis=0).astype(bf16)
    last, mlp = lax.optimization_barrier((last, mlp))
    mlp = lax.psum_scatter(mlp, "x", scatter_dimension=0, tiled=True)
    ends = lax.all_to_all(jnp.broadcast_to(last[None], (64, 17, 128)), CHIPS, 0, 0, tiled=True)
    d_win = contract(pooled, got[:, 16:32].reshape(1024, 128), (0,), (0,))
    ends, d_win = lax.optimization_barrier((ends, d_win))
    ends = in_order(c, ends, lax.ppermute(ends, "c", SWAP)).astype(f32)
    values = ends[:, :, :16].reshape(vocab, width)
    d_lat = ends[:, :16, 16].transpose(1, 0, 2).reshape(latd)
    d_enc = jnp.sum(values * unit, axis=0)
    scaled_e = values * enc_gain
    d_emb = enc_rms * (scaled_e - unit * jnp.mean(scaled_e * unit, axis=-1, keepdims=True))

    rows = (lat_own + mlp.astype(f32)).astype(bf16).reshape(2, 8, 2048)
    rows = in_order(c, mine_of(rows, c, 0), lax.ppermute(mine_of(rows, 1 - c, 0), "c", SWAP))
    patch_out = rows.reshape(2, 8, 16, 128).transpose(1, 2, 0, 3).reshape(1, 1, 8, latd)
    return (patch_out, d_emb, d_enc, d_win, d_lat, d_wg, d_wu, d_wd)


def solution(mesh):
    fine = Mesh(mesh.devices.reshape(4, 4, 4, 2), ALL)
    seq = ("z", "x", "c")
    ff = P(ALL, None)
    return jax.shard_map(
        on_device,
        mesh=fine,
        in_specs=(
            P("y", seq), P("y", None), P("y", None), P(), P(), P(None, seq), P(),
            ff, ff, ff, P("y", seq, None, None),
        ),
        out_specs=(P("y", seq, None, None), P(), P(), P(None, seq), P(), ff, ff, ff),
        check_vma=False,
    )
```

```python
import jax
import jax.numpy as jnp
from jax import lax
from jax.experimental import pallas as pl
from jax.experimental.pallas import tpu as pltpu
from jax.sharding import Mesh, PartitionSpec as P

ALL = ("y", "z", "x", "c")
CHIPS = ("y", "z", "x")
SWAP = [(0, 1), (1, 0)]
EPS = 1e-05
bf16 = jnp.bfloat16
f32 = jnp.float32


def rms_scale(values):
    return lax.rsqrt(jnp.mean(values * values, axis=-1, keepdims=True) + EPS)


def silu_parts(gate):
    sigma = jax.nn.sigmoid(gate)
    return (gate * sigma, sigma * (1.0 + gate * (1.0 - sigma)))


def owner_slots(lengths, owners):
    onehot_own = (owners[:, None] == jnp.arange(32, dtype=jnp.int32)[None, :]).astype(jnp.int32)
    rank = jnp.sum((jnp.cumsum(onehot_own, axis=0) - onehot_own) * onehot_own, axis=1)
    target = owners * 8 + rank
    placed = target[None, :] == jnp.arange(256, dtype=jnp.int32)[:, None]
    starts = jnp.cumsum(lengths) - lengths
    slot_start = jnp.sum(jnp.where(placed, starts[None, :], 0), axis=1)
    slot_len = jnp.sum(jnp.where(placed, lengths[None, :], 0), axis=1)
    return (slot_start, slot_len)


def slot_counts(ids, lengths, owners, vocab):
    slot_start, slot_len = owner_slots(lengths, owners)
    position = jnp.arange(ids.shape[0], dtype=jnp.int32)
    member = (position[None, :] >= slot_start[:, None]) & (
        position[None, :] < (slot_start + slot_len)[:, None]
    )
    onehot = ids[:, None] == jnp.arange(vocab, dtype=jnp.int32)[None, :]
    counts = jnp.dot(member.astype(bf16), onehot.astype(bf16), preferred_element_type=f32)
    return counts, slot_len


def contract(left, right, left_dims, right_dims):
    return lax.dot_general(
        left, right, ((left_dims, right_dims), ((), ())), preferred_element_type=f32
    )


def first_kernel(win_blocks, cot_blocks, pooled, w_gu, w_dn, gain, lat_out, cot_out, part_out, win):
    step = pl.program_id(0)

    @pl.when(step == 0)
    def _():
        for y in range(4):
            for block in range(16):
                win[y * 256:(y + 1) * 256, block * 128:(block + 1) * 128] = (
                    win_blocks[y * 16 + block, :, :]
                )

    for chip in range(16):
        for block in range(16):
            cot_out[chip * 16:(chip + 1) * 16, block * 128:(block + 1) * 128] = (
                cot_blocks[chip, block * 16:(block + 1) * 16, :]
            )
    latent = jnp.dot(pooled[...], win[...], preferred_element_type=f32).astype(bf16)
    lat_out[...] = latent
    lat32 = latent.astype(f32)
    scaled = (lat32 * gain[...]).astype(bf16)
    part_out[0, 0:448, :] = contract(w_gu[...], scaled, (1,), (1,)).astype(bf16)
    part_out[0, 448:672, :] = contract(w_dn[...], cot_out[...], (1,), (1,)).astype(bf16)
    squares = contract(
        jnp.ones((16, 2048), bf16), (lat32 * lat32).astype(bf16), (1,), (1,)
    )
    high = squares.astype(bf16).astype(f32)
    top = lax.broadcasted_iota(jnp.int32, squares.shape, 0) < 8
    part_out[0, 672:688, :] = jnp.where(top, high, squares - high).astype(bf16)


def first_products(whole, pooled, w_gu, w_dn, gain):
    once = pl.Buffered(1)
    fixed = lambda *shape: pl.BlockSpec(shape, lambda i: (0,) * len(shape), pipeline_mode=once)
    rows = lambda width: pl.BlockSpec((256, width), lambda i: (i, 0))
    return pl.pallas_call(
        first_kernel,
        grid=(4,),
        in_specs=[
            fixed(64, 256, 128), pl.BlockSpec((16, 256, 128), lambda i: (i, 1, 0)), rows(1024),
            fixed(448, 2048), fixed(224, 2048), fixed(1, 2048),
        ],
        out_specs=[
            rows(2048), rows(2048),
            pl.BlockSpec((1, 688, 256), lambda i: (i // 2, 0, i % 2)),
            pl.BlockSpec((1024, 2048), lambda i: (0, 0), pipeline_mode=once),
        ],
        out_shape=[
            jax.ShapeDtypeStruct((1024, 2048), bf16),
            jax.ShapeDtypeStruct((1024, 2048), bf16),
            jax.ShapeDtypeStruct((2, 688, 512), bf16),
            jax.ShapeDtypeStruct((1024, 2048), bf16),
        ],
        compiler_params=pltpu.CompilerParams(vmem_limit_bytes=56 * 2**20),
        cost_estimate=pl.CostEstimate(
            flops=2 * 1024 * 2048 * (1024 + 688), bytes_accessed=30 * 2**20, transcendentals=0
        ),
    )(whole, whole, pooled, w_gu, w_dn, gain)


def second_kernel(place, acts, w_gu, latent, gain, cot_own, counts, win, dl_out, value_out, d_lat_out, dl, by_value):
    step = pl.program_id(0)
    lat32 = latent[...].astype(f32)
    part = contract(acts[0, 0:448, :], w_gu[...], (0,), (0,))

    @pl.when(step == 0)
    def _():
        by_value[...] = jnp.zeros_like(by_value)
        d_lat_out[...] = jnp.zeros_like(d_lat_out)

    d_lat_out[...] += jnp.sum(part * lat32, axis=0, keepdims=True)
    pick = jnp.where(lax.broadcasted_iota(jnp.int32, (16, 128), 0) < 2, 1.0, 0.0).astype(bf16)
    mean_rows = contract(acts[0, 672:688, :], pick, (0,), (0,))[:, 0:1]
    dl[...] = part * gain[...] - mean_rows * lat32

    @pl.when(step == place[0])
    def _():
        rows = pl.ds(pl.multiple_of(place[1] * 16, 16), 16)
        dl[rows, :] += cot_own[...].astype(f32)

    dlatent = dl[...].astype(bf16)
    for block in range(16):
        dl_out[block, :, :] = dlatent[:, block * 128:(block + 1) * 128]
    by_value[...] += contract(counts[...], dlatent, (0,), (0,))

    @pl.when(step == 3)
    def _():
        value_out[...] = contract(by_value[...].astype(bf16), win[...], (1,), (1,)).astype(bf16)


def second_products(place, acts, w_gu, latent, gain, cot_own, counts, win):
    once = pl.Buffered(1)
    fixed = lambda *shape: pl.BlockSpec(shape, lambda i, p: (0,) * len(shape), pipeline_mode=once)
    rows = lambda width: pl.BlockSpec((256, width), lambda i, p: (i, 0))
    return pl.pallas_call(
        second_kernel,
        grid_spec=pltpu.PrefetchScalarGridSpec(
            num_scalar_prefetch=1,
            grid=(4,),
            in_specs=[
                pl.BlockSpec((1, 688, 256), lambda i, p: (i // 2, 0, i % 2)),
                fixed(448, 2048), rows(2048), fixed(1, 2048), fixed(16, 2048), rows(256),
                fixed(1024, 2048),
            ],
            out_specs=[
                pl.BlockSpec((16, 256, 128), lambda i, p: (i, 0, 0)),
                fixed(256, 1024),
                fixed(1, 2048),
            ],
            scratch_shapes=[pltpu.VMEM((256, 2048), f32), pltpu.VMEM((256, 2048), f32)],
        ),
        out_shape=[
            jax.ShapeDtypeStruct((64, 288, 128), bf16),
            jax.ShapeDtypeStruct((256, 1024), bf16),
            jax.ShapeDtypeStruct((1, 2048), f32),
        ],
        compiler_params=pltpu.CompilerParams(vmem_limit_bytes=56 * 2**20),
        cost_estimate=pl.CostEstimate(
            flops=2 * 256 * 2048 * (4 * (448 + 256) + 1024), bytes_accessed=18 * 2**20,
            transcendentals=0,
        ),
    )(place, acts, w_gu, latent, gain, cot_own, counts, win)


def after(value, other):
    return value + (other.reshape(-1)[0] * 0).astype(value.dtype)


def in_order(core, own, came):
    return jnp.stack([jnp.where(core == 0, own, came), jnp.where(core == 0, came, own)])


def on_device(
    byte_ids, patch_lengths, patch_owner, emb_table, enc_gain, w_in, lat_gain,
    w_gate, w_up, w_down, grad_out,
):
    y, z, x, c = (lax.axis_index(a) for a in ALL)
    chip = z * 4 + x
    seq = chip * 2 + c
    vocab, width = emb_table.shape
    latd = lat_gain.shape[0]
    mine_of = lambda a, which, axis: lax.dynamic_index_in_dim(a, which, axis, keepdims=False)

    cot_parts = grad_out[0, 0].reshape(8, 16, 2, 128)
    cot_came = lax.ppermute(mine_of(cot_parts, 1 - c, 2), "c", SWAP)
    cot_chip = in_order(c, mine_of(cot_parts, c, 2), cot_came)
    cot_own = cot_chip.reshape(16, 2048)
    cot_chip = cot_chip.reshape(16, 16, 128).transpose(1, 0, 2).reshape(256, 128)
    win_quarter = lax.dynamic_slice_in_dim(w_in, y * 256, 256, 0)
    whole = lax.all_gather(
        jnp.concatenate([win_quarter, cot_chip], axis=0)[None], CHIPS, axis=0, tiled=True
    )

    tiny = jnp.concatenate(
        [
            byte_ids[0],
            lax.dynamic_slice_in_dim(patch_lengths[0], seq * 8, 8),
            lax.dynamic_slice_in_dim(patch_owner[0], seq * 8, 8),
            jnp.zeros((112,), jnp.int32),
        ]
    )
    tiny_all = lax.all_to_all(
        jnp.broadcast_to(tiny.reshape(1, 2, 128), (128, 2, 128)), ALL, 0, 0, tiled=True
    )
    ids = tiny_all[:, 0].reshape(4, 4096)
    lengths = tiny_all[:, 1, :8].reshape(4, 256)
    owners = tiny_all[:, 1, 8:16].reshape(4, 256)

    weights = jnp.stack([w_gate, w_up, w_down]).reshape(3, 112, 16, 2, 128)
    weights_own = mine_of(weights, c, 3).reshape(3, 112, 2048)
    weights_came = lax.ppermute(mine_of(weights, 1 - c, 3).reshape(3, 112, 2048), "c", SWAP)
    weights = in_order(c, weights_own, weights_came).transpose(1, 0, 2, 3)
    w_gu = weights[:2].reshape(448, 2048)
    w_dn = weights[2].reshape(224, 2048)

    embedded = emb_table.astype(f32)
    enc_rms = rms_scale(embedded)
    unit = embedded * enc_rms
    table = (unit * enc_gain).astype(bf16)
    counts, slot_len = jax.vmap(lambda i, n, o: slot_counts(i, n, o, vocab))(ids, lengths, owners)
    counts = counts.reshape(1024, vocab)
    lens = slot_len.reshape(1024, 1).astype(f32)
    pooled = (jnp.dot(counts.astype(bf16), table, preferred_element_type=f32) / lens).astype(bf16)
    shares = (counts / lens).astype(bf16)
    place = jnp.stack([y, chip]).astype(jnp.int32)
    pooled, shares, place = lax.optimization_barrier((pooled, shares, place))
    gain = mine_of(lat_gain.reshape(16, 2, 128), c, 1).reshape(1, 2048)

    latent, cot, part, win = first_products(whole, pooled, w_gu, w_dn, gain)
    part_came = lax.ppermute(mine_of(part, 1 - c, 0), "c", SWAP)
    total = mine_of(part, c, 0).astype(f32) + part_came.astype(f32)

    gate0 = total[:224]
    up0 = total[224:448]
    dhid = total[448:672]
    rms = lax.rsqrt((total[672:673] + total[680:681]) / latd + EPS)
    upper = up0 * rms
    active, slope = silu_parts(gate0 * rms)
    dgate = dhid * upper * slope * rms
    dup = dhid * active * rms
    mean_rows = jnp.sum(dgate * gate0 + dup * up0, axis=0, keepdims=True) * (rms * rms / latd)
    mean_high = mean_rows.astype(bf16).astype(f32)
    acts = jnp.concatenate(
        [
            dgate, dup, active * upper, mean_high, mean_rows - mean_high,
            jnp.zeros((14, 512), f32),
        ],
        axis=0,
    ).astype(bf16)
    acts = in_order(c, acts, lax.ppermute(acts, "c", SWAP))
    dgu = acts[:, :448]
    hidden = acts[:, 448:672]

    dl_part, value_part, d_lat_part = second_products(
        place, acts, w_gu, latent, gain, cot_own, shares, win
    )
    value_part = value_part.reshape(2, 64, 16, 128)
    value_came = lax.ppermute(mine_of(value_part, 1 - c, 0), "c", SWAP)
    mlp = contract(hidden, w_dn, (1,), (0,)).astype(bf16).reshape(1024, 2048)
    value_came, mlp = lax.optimization_barrier((value_came, mlp))
    mlp = lax.psum_scatter(mlp, "y", scatter_dimension=0, tiled=True)
    value_half = (mine_of(value_part, c, 0).astype(f32) + value_came.astype(f32)).astype(bf16)
    d_lat_part = jnp.broadcast_to(
        d_lat_part.astype(bf16).reshape(1, 16, 1, 128), (4, 16, 1, 128)
    ).reshape(64, 1, 128)
    extra = jnp.concatenate([value_half, d_lat_part, jnp.zeros((64, 15, 128), bf16)], axis=1)
    sent = lax.dynamic_update_slice(dl_part, extra, (0, 256, 0))
    sent, dgu, hidden = lax.optimization_barrier((sent, dgu, hidden))
    got = lax.all_to_all(sent, CHIPS, 0, 0, tiled=True)

    d_gu = contract(dgu, latent.reshape(2, 512, 2048), (0, 2), (0, 1)) * gain
    d_dn = contract(hidden, cot.reshape(2, 512, 2048), (0, 2), (0, 1))
    d_weights = jnp.concatenate([d_gu, d_dn], axis=0).reshape(3, 2, 112, 2048)
    d_own = mine_of(d_weights, c, 1)
    d_came = lax.ppermute(mine_of(d_weights, 1 - c, 1), "c", SWAP)
    d_weights = in_order(c, d_own, d_came).reshape(2, 3, 112, 16, 128).transpose(1, 2, 3, 0, 4)
    d_wg, d_wu, d_wd = d_weights.reshape(3, 112, latd)
    got, d_wg, d_wu, d_wd = lax.optimization_barrier((got, d_wg, d_wu, d_wd))
    sums = jnp.sum(got.astype(f32), axis=0)

    last = sums[256:273].astype(bf16)
    ends = lax.all_to_all(jnp.broadcast_to(last[None], (64, 17, 128)), CHIPS, 0, 0, tiled=True)
    dlatent = after(sums[:256].astype(bf16), ends[0, 0, 0])
    pooled_rows = pooled.reshape(4, 256, width)
    d_win = contract(mine_of(pooled_rows, y, 0), dlatent, (0,), (0,))
    for shift in (1, 2, 3):
        came = lax.ppermute(dlatent, "y", [(i, (i + shift) % 4) for i in range(4)])
        d_win += contract(mine_of(pooled_rows, (y - shift) % 4, 0), came, (0,), (0,))
    ends, mlp = lax.optimization_barrier((ends, mlp))
    mlp = lax.all_to_all(mlp.reshape(16, 16, 2048), ("z", "x"), 0, 0, tiled=True)
    mlp = jnp.sum(mlp.astype(f32), axis=0)
    ends = in_order(c, ends, lax.ppermute(ends, "c", SWAP)).astype(f32)
    values = ends[:, :, :16].reshape(vocab, width)
    d_lat = ends[:, :16, 16].transpose(1, 0, 2).reshape(latd)
    d_enc = jnp.sum(values * unit, axis=0)
    scaled_e = values * enc_gain
    d_emb = enc_rms * (scaled_e - unit * jnp.mean(scaled_e * unit, axis=-1, keepdims=True))

    row0 = (y * 16 + chip) * 16
    lat_own = lax.dynamic_slice_in_dim(latent, row0, 16, 0).astype(f32)
    rows = (lat_own + mlp).astype(bf16).reshape(2, 8, 2048)
    rows = in_order(c, mine_of(rows, c, 0), lax.ppermute(mine_of(rows, 1 - c, 0), "c", SWAP))
    patch_out = rows.reshape(2, 8, 16, 128).transpose(1, 2, 0, 3).reshape(1, 1, 8, latd)
    return (patch_out, d_emb, d_enc, d_win, d_lat, d_wg, d_wu, d_wd)


def solution(mesh):
    fine = Mesh(mesh.devices.reshape(4, 4, 4, 2), ALL)
    seq = ("z", "x", "c")
    ff = P(ALL, None)
    return jax.shard_map(
        on_device,
        mesh=fine,
        in_specs=(
            P("y", seq), P("y", None), P("y", None), P(), P(), P(None, seq), P(),
            ff, ff, ff, P("y", seq, None, None),
        ),
        out_specs=(P("y", seq, None, None), P(), P(), P(None, seq), P(), ff, ff, ff),
        check_vma=False,
    )
```

```python
import jax
import jax.numpy as jnp
from jax import lax
from jax.experimental import pallas as pl
from jax.experimental.pallas import tpu as pltpu
from jax.sharding import Mesh, PartitionSpec as P

ALL = ("y", "z", "x", "c")
CHIPS = ("y", "z", "x")
SWAP = [(0, 1), (1, 0)]
EPS = 1e-05
bf16 = jnp.bfloat16
f32 = jnp.float32


def rms_scale(values):
    return lax.rsqrt(jnp.mean(values * values, axis=-1, keepdims=True) + EPS)


def silu_parts(gate):
    sigma = jax.nn.sigmoid(gate)
    return (gate * sigma, sigma * (1.0 + gate * (1.0 - sigma)))


def owner_slots(lengths, owners):
    onehot_own = (owners[:, None] == jnp.arange(32, dtype=jnp.int32)[None, :]).astype(jnp.int32)
    rank = jnp.sum((jnp.cumsum(onehot_own, axis=0) - onehot_own) * onehot_own, axis=1)
    target = owners * 8 + rank
    placed = target[None, :] == jnp.arange(256, dtype=jnp.int32)[:, None]
    starts = jnp.cumsum(lengths) - lengths
    slot_start = jnp.sum(jnp.where(placed, starts[None, :], 0), axis=1)
    slot_len = jnp.sum(jnp.where(placed, lengths[None, :], 0), axis=1)
    return (slot_start, slot_len)


def slot_counts(ids, lengths, owners, vocab):
    slot_start, slot_len = owner_slots(lengths, owners)
    position = jnp.arange(ids.shape[0], dtype=jnp.int32)
    member = (position[None, :] >= slot_start[:, None]) & (
        position[None, :] < (slot_start + slot_len)[:, None]
    )
    onehot = ids[:, None] == jnp.arange(vocab, dtype=jnp.int32)[None, :]
    counts = jnp.dot(member.astype(bf16), onehot.astype(bf16), preferred_element_type=f32)
    return counts, slot_len


def contract(left, right, left_dims, right_dims):
    return lax.dot_general(
        left, right, ((left_dims, right_dims), ((), ())), preferred_element_type=f32
    )


def first_kernel(win_blocks, cot_blocks, pooled, w_gu, w_dn, gain, lat_out, cot_out, part_out, win):
    step = pl.program_id(0)

    @pl.when(step == 0)
    def _():
        for y in range(4):
            for block in range(16):
                win[y * 256:(y + 1) * 256, block * 128:(block + 1) * 128] = (
                    win_blocks[y * 16 + block, :, :]
                )

    for chip in range(16):
        for block in range(16):
            cot_out[chip * 16:(chip + 1) * 16, block * 128:(block + 1) * 128] = (
                cot_blocks[chip, block * 16:(block + 1) * 16, :]
            )
    latent = jnp.dot(pooled[...], win[...], preferred_element_type=f32).astype(bf16)
    lat_out[...] = latent
    lat32 = latent.astype(f32)
    scaled = (lat32 * gain[...]).astype(bf16)
    part_out[0, 0:448, :] = contract(w_gu[...], scaled, (1,), (1,)).astype(bf16)
    part_out[0, 448:672, :] = contract(w_dn[...], cot_out[...], (1,), (1,)).astype(bf16)
    squares = contract(
        jnp.ones((16, 2048), bf16), (lat32 * lat32).astype(bf16), (1,), (1,)
    )
    high = squares.astype(bf16).astype(f32)
    top = lax.broadcasted_iota(jnp.int32, squares.shape, 0) < 8
    part_out[0, 672:688, :] = jnp.where(top, high, squares - high).astype(bf16)


def first_products(whole, pooled, w_gu, w_dn, gain):
    once = pl.Buffered(1)
    fixed = lambda *shape: pl.BlockSpec(shape, lambda i: (0,) * len(shape), pipeline_mode=once)
    rows = lambda width: pl.BlockSpec((256, width), lambda i: (i, 0))
    return pl.pallas_call(
        first_kernel,
        grid=(4,),
        in_specs=[
            fixed(64, 256, 128), pl.BlockSpec((16, 256, 128), lambda i: (i, 1, 0)), rows(1024),
            fixed(448, 2048), fixed(224, 2048), fixed(1, 2048),
        ],
        out_specs=[
            rows(2048), rows(2048),
            pl.BlockSpec((1, 688, 256), lambda i: (i // 2, 0, i % 2)),
            pl.BlockSpec((1024, 2048), lambda i: (0, 0), pipeline_mode=once),
        ],
        out_shape=[
            jax.ShapeDtypeStruct((1024, 2048), bf16),
            jax.ShapeDtypeStruct((1024, 2048), bf16),
            jax.ShapeDtypeStruct((2, 688, 512), bf16),
            jax.ShapeDtypeStruct((1024, 2048), bf16),
        ],
        compiler_params=pltpu.CompilerParams(vmem_limit_bytes=56 * 2**20),
        cost_estimate=pl.CostEstimate(
            flops=2 * 1024 * 2048 * (1024 + 688), bytes_accessed=30 * 2**20, transcendentals=0
        ),
    )(whole, whole, pooled, w_gu, w_dn, gain)


def after(value, other):
    return value + (other * 0).astype(value.dtype)


def in_order(core, own, came):
    return jnp.stack([jnp.where(core == 0, own, came), jnp.where(core == 0, came, own)])


def on_device(
    byte_ids, patch_lengths, patch_owner, emb_table, enc_gain, w_in, lat_gain,
    w_gate, w_up, w_down, grad_out,
):
    y, z, x, c = (lax.axis_index(a) for a in ALL)
    chip = z * 4 + x
    seq = chip * 2 + c
    vocab, width = emb_table.shape
    latd = lat_gain.shape[0]
    mine_of = lambda a, which, axis: lax.dynamic_index_in_dim(a, which, axis, keepdims=False)

    cot_parts = grad_out[0, 0].reshape(8, 16, 2, 128)
    cot_came = lax.ppermute(mine_of(cot_parts, 1 - c, 2), "c", SWAP)
    cot_chip = in_order(c, mine_of(cot_parts, c, 2), cot_came)
    cot_chip = cot_chip.reshape(16, 16, 128).transpose(1, 0, 2).reshape(256, 128)
    win_quarter = lax.dynamic_slice_in_dim(w_in, y * 256, 256, 0)
    whole = lax.all_gather(
        jnp.concatenate([win_quarter, cot_chip], axis=0)[None], CHIPS, axis=0, tiled=True
    )

    tiny = jnp.concatenate(
        [
            byte_ids[0],
            lax.dynamic_slice_in_dim(patch_lengths[0], seq * 8, 8),
            lax.dynamic_slice_in_dim(patch_owner[0], seq * 8, 8),
            jnp.zeros((112,), jnp.int32),
        ]
    )
    tiny_all = lax.all_to_all(
        jnp.broadcast_to(tiny.reshape(1, 2, 128), (128, 2, 128)), ALL, 0, 0, tiled=True
    )
    ids = tiny_all[:, 0].reshape(4, 4096)
    lengths = tiny_all[:, 1, :8].reshape(4, 256)
    owners = tiny_all[:, 1, 8:16].reshape(4, 256)

    weights = jnp.stack([w_gate, w_up, w_down]).reshape(3, 112, 16, 2, 128)
    weights_own = mine_of(weights, c, 3).reshape(3, 112, 2048)
    weights_came = lax.ppermute(mine_of(weights, 1 - c, 3).reshape(3, 112, 2048), "c", SWAP)
    weights = in_order(c, weights_own, weights_came).transpose(1, 0, 2, 3)
    w_gu = weights[:2].reshape(448, 2048)
    w_dn = weights[2].reshape(224, 2048)

    embedded = emb_table.astype(f32)
    enc_rms = rms_scale(embedded)
    unit = embedded * enc_rms
    table = (unit * enc_gain).astype(bf16)
    counts, slot_len = jax.vmap(lambda i, n, o: slot_counts(i, n, o, vocab))(ids, lengths, owners)
    counts = counts.reshape(1024, vocab)
    lens = slot_len.reshape(1024, 1).astype(f32)
    pooled = (jnp.dot(counts.astype(bf16), table, preferred_element_type=f32) / lens).astype(bf16)
    gain = mine_of(lat_gain.reshape(16, 2, 128), c, 1).reshape(1, 2048)

    latent, cot, part, win = first_products(whole, pooled, w_gu, w_dn, gain)
    part_came = lax.ppermute(mine_of(part, 1 - c, 0), "c", SWAP)
    total = mine_of(part, c, 0).astype(f32) + part_came.astype(f32)

    gate0 = total[:224]
    up0 = total[224:448]
    dhid = total[448:672]
    rms = lax.rsqrt((total[672:673] + total[680:681]) / latd + EPS)
    upper = up0 * rms
    active, slope = silu_parts(gate0 * rms)
    acts = jnp.concatenate(
        [dhid * upper * slope * rms, dhid * active * rms, active * upper], axis=0
    ).astype(bf16)
    acts = in_order(c, acts, lax.ppermute(acts, "c", SWAP))
    dgu = acts[:, :448]
    hidden = acts[:, 448:]

    dn_part = contract(dgu, w_gu, (1,), (0,)).astype(bf16)
    dn_sent = lax.all_to_all(dn_part.reshape(64, 16, 2048), CHIPS, 0, 0, tiled=True)
    mlp = contract(hidden, w_dn, (1,), (0,)).astype(bf16).reshape(1024, 2048)
    mlp = lax.psum_scatter(mlp, "y", scatter_dimension=0, tiled=True)

    d_gu = contract(dgu, latent.reshape(2, 512, 2048), (0, 2), (0, 1)) * gain
    d_dn = contract(hidden, cot.reshape(2, 512, 2048), (0, 2), (0, 1))
    d_weights = jnp.concatenate([d_gu, d_dn], axis=0).reshape(3, 2, 112, 2048)
    d_own = mine_of(d_weights, c, 1)
    d_came = lax.ppermute(mine_of(d_weights, 1 - c, 1), "c", SWAP)
    d_weights = in_order(c, d_own, d_came).reshape(2, 3, 112, 16, 128).transpose(1, 2, 3, 0, 4)
    d_wg, d_wu, d_wd = d_weights.reshape(3, 112, latd)
    dn_sent, d_wg, d_wu, d_wd = lax.optimization_barrier((dn_sent, d_wg, d_wu, d_wd))
    dnormed = jnp.sum(dn_sent.astype(f32), axis=0)

    row0 = (y * 16 + chip) * 16
    lat_own = lax.dynamic_slice_in_dim(latent, row0, 16, 0).astype(f32)
    cot_own = lax.dynamic_slice_in_dim(cot, row0, 16, 0).astype(f32)
    scaled = dnormed * gain
    sums = jnp.stack([jnp.sum(scaled * lat_own, axis=1), jnp.sum(lat_own * lat_own, axis=1)])
    sums = (sums + lax.ppermute(sums, "c", SWAP)) / latd
    mean_rows = sums[0][:, None] / (sums[1][:, None] + EPS)
    dlatent = (cot_own + scaled - lat_own * mean_rows).astype(bf16)
    d_lat_part = jnp.sum(dnormed * lat_own, axis=0)

    dpool = contract(dlatent, win, (1,), (1,)) / lax.dynamic_slice_in_dim(lens, row0, 16, 0)
    value_part = lax.dot_general(
        lax.dynamic_slice_in_dim(counts, row0, 16, 0), dpool, (((0,), (0,)), ((), ())),
        precision=lax.Precision.HIGHEST, preferred_element_type=f32,
    ).astype(bf16).reshape(2, 64, 16, 128)
    value_came = lax.ppermute(mine_of(value_part, 1 - c, 0), "c", SWAP)
    value_half = (mine_of(value_part, c, 0).astype(f32) + value_came.astype(f32)).astype(bf16)
    columns = jnp.concatenate(
        [dlatent.reshape(16, 16, 128), d_lat_part.astype(bf16).reshape(1, 16, 128)], axis=0
    ).transpose(1, 0, 2)
    columns = jnp.broadcast_to(columns[None], (4, 16, 17, 128)).reshape(64, 17, 128)
    sent = jnp.concatenate([value_half, columns], axis=1)
    sent, mlp = lax.optimization_barrier((sent, mlp))
    mlp = lax.psum_scatter(mlp, "z", scatter_dimension=0, tiled=True)
    got = lax.all_to_all(sent, CHIPS, 0, 0, tiled=True)
    values = jnp.sum(got[:, :16].astype(f32), axis=0)
    d_lat_own = jnp.sum(got[:, 32].astype(f32), axis=0)

    last = jnp.concatenate([values, d_lat_own[None]], axis=0).astype(bf16)
    ends = lax.all_to_all(jnp.broadcast_to(last[None], (64, 17, 128)), CHIPS, 0, 0, tiled=True)
    mlp = after(mlp, ends[0, 0, 0]).reshape(4, 16, 2048)
    mlp = jnp.sum(lax.all_to_all(mlp, "x", 0, 0, tiled=True).astype(f32), axis=0)
    d_win = contract(pooled, got[:, 16:32].reshape(1024, 128), (0,), (0,))
    ends, d_win = lax.optimization_barrier((ends, d_win))
    ends = in_order(c, ends, lax.ppermute(ends, "c", SWAP)).astype(f32)
    values = ends[:, :, :16].reshape(vocab, width)
    d_lat = ends[:, :16, 16].transpose(1, 0, 2).reshape(latd)
    d_enc = jnp.sum(values * unit, axis=0)
    scaled_e = values * enc_gain
    d_emb = enc_rms * (scaled_e - unit * jnp.mean(scaled_e * unit, axis=-1, keepdims=True))

    rows = (lat_own + mlp).astype(bf16).reshape(2, 8, 2048)
    rows = in_order(c, mine_of(rows, c, 0), lax.ppermute(mine_of(rows, 1 - c, 0), "c", SWAP))
    patch_out = rows.reshape(2, 8, 16, 128).transpose(1, 2, 0, 3).reshape(1, 1, 8, latd)
    return (patch_out, d_emb, d_enc, d_win, d_lat, d_wg, d_wu, d_wd)


def solution(mesh):
    fine = Mesh(mesh.devices.reshape(4, 4, 4, 2), ALL)
    seq = ("z", "x", "c")
    ff = P(ALL, None)
    return jax.shard_map(
        on_device,
        mesh=fine,
        in_specs=(
            P("y", seq), P("y", None), P("y", None), P(), P(), P(None, seq), P(),
            ff, ff, ff, P("y", seq, None, None),
        ),
        out_specs=(P("y", seq, None, None), P(), P(), P(None, seq), P(), ff, ff, ff),
        check_vma=False,
    )
```
